32 devices in a mesh: row: 4 (over z), col: 4 (over y, core), mode: 2 (over x).
Axes of the slice: x: 2, y: 2, z: 4, core: 2. Of those that a mesh axis runs over, the one named last changes fastest.
Arguments:
- objects: float32 [2, 2, 1024, 1024], P(None, None, 'row', 'col'), may hold values from -4 to 4
- probes: float32 [2, 2, 128, 128], P('mode'), may hold values from -3 to 3
- phase: float32 [128, 128], replicated, may hold values from -3.140625 to 3.140625
- offsets: int32 [4, 4, 8, 2], P('row', 'col'), may hold values from 0 to 255
- measured: float32 [4, 4, 8, 128, 128], P('row', 'col'), may hold values from 0 to 2
Outputs:
- gradient: float32 [2, 2, 1024, 1024], P(None, None, 'row', 'col')
The draws below stay inside these ranges and needn't reach their ends.
Inputs may be any that keep to these rules, and one draw needn't show every extreme that they name: `offsets`: windows start inside their own tile of 256 x 256 cells and reach up to 127 cells into the next tiles down and to the right.
All inputs are finite; a program needn't handle non-finite values.
Results may differ from the reference program's by a relative error of at most 0.0001.
Values sent between devices are 32-bit elements; how exact they have to be, the bound alone decides.
No kernel may reach another device: no remote copies, remote signals or barrier semaphores. Data moves between devices by JAX's collectives and lax.ppermute only.
A program may use at most 64 MiB of HBM per device.

```python
import jax
import jax.numpy as jnp
from jax import lax

TILE = 256
POS = 8
WIN = 128
SLICES = 2
MODES = 2
NR = 1024
NC = 1024
TR = 4
TC = 4
N_ROW = 4
N_COL = 4


def plant(result, own_key, least, largest):
    longest = result.shape.index(max(result.shape))
    spots = []
    for shift in (0, 1):
        where = [jax.random.randint(jax.random.fold_in(own_key, axis), (), 0, length) for axis, length in enumerate(result.shape)]
        where[longest] = (where[longest] + shift) % result.shape[longest]
        spots.append(tuple(where))
    return result.at[spots[0]].set(least).at[spots[1]].set(largest)


def block_levels(stream_key, dims, shards, least, largest):
    factor_of, own = 1.0, jax.random.fold_in(stream_key, 6)
    for axis_at, blocks in shards:
        draws = jnp.exp(jax.random.uniform(jax.random.fold_in(own, axis_at), (blocks,), jnp.float32, least / len(shards), largest / len(shards)))
        factor_of = factor_of * jnp.repeat(draws, dims[axis_at] // blocks).reshape([-1 if axis == axis_at else 1 for axis in range(len(dims))])
    return factor_of


def scatter_about(own_key, extent, scale, reach, shards=(), kind=jnp.bfloat16):
    array = jax.random.normal(own_key, extent, jnp.float32) * scale
    if len(shards) > 0:
        array = block_levels(own_key, extent, shards, -0.22, 0.18) * array
    return jnp.clip(array, min=-reach, max=reach).astype(kind)


def setup_inputs(seed: int = 0) -> dict:
    splits = jax.random.split(jax.random.key(seed), 6)
    return {
        "objects": scatter_about(splits[0], (SLICES, 2, NR, NC), 0.7, 4.0, ((2, 4), (3, 4)), jnp.float32),
        "probes": scatter_about(splits[1], (MODES, 2, WIN, WIN), 0.5, 3.0, ((0, 2),), jnp.float32),
        "phase": jnp.clip(jax.random.uniform(splits[2], (WIN, WIN), jnp.float32, -3.140625, 3.140625), -3.140625, 3.140625),
        "offsets": plant(jax.random.randint(splits[3], (TR, TC, POS, 2), 0, TILE), jax.random.fold_in(splits[3], 1), 0, TILE - 1).astype(jnp.int32),
        "measured": jnp.clip(2.0 * jax.random.uniform(splits[4], (TR, TC, POS, WIN, WIN), jnp.float32) ** block_levels(splits[4], (TR, TC, POS, WIN, WIN), ((0, 4), (1, 4)), -0.2, 0.2), 0.0, 2.0),
    }


def forward_two(field):
    return jnp.fft.fft2(field, norm="ortho")


def inverse_two(field):
    return jnp.fft.ifft2(field, norm="ortho")


def reference(objects, probes, phase, offsets, measured):
    object_c = objects[:, 0] + 1j * objects[:, 1]
    padded = jnp.pad(object_c, ((0, 0), (0, WIN), (0, WIN)))
    probe_c = probes[:, 0] + 1j * probes[:, 1]
    propagator = jnp.cos(phase) + 1j * jnp.sin(phase)
    tile_rows = (jnp.arange(N_ROW, dtype=jnp.int32) * TILE)[:, None, None]
    tile_cols = (jnp.arange(N_COL, dtype=jnp.int32) * TILE)[None, :, None]
    start_rows = (offsets[..., 0].astype(jnp.int32) + tile_rows).reshape(-1)
    start_cols = (offsets[..., 1].astype(jnp.int32) + tile_cols).reshape(-1)
    measured_flat = measured.reshape(-1, WIN, WIN)
    zero_index = jnp.int32(0)

    def advance(carry, item):
        row_start, col_start, target = item
        window = lax.dynamic_slice(padded, (zero_index, row_start, col_start), (SLICES, WIN, WIN))
        first = probe_c * window[0]
        middle = inverse_two(propagator * forward_two(first))
        exit_wave = middle * window[1]
        far_field = forward_two(exit_wave)
        intensity = jnp.sum(jnp.abs(far_field) ** 2, axis=0)
        resid = intensity - target
        grad_far = 4.0 * resid * far_field
        grad_exit = inverse_two(grad_far)
        grad_second = jnp.sum(grad_exit * jnp.conj(middle), axis=0)
        grad_middle = grad_exit * jnp.conj(window[1])
        grad_first = inverse_two(jnp.conj(propagator) * forward_two(grad_middle))
        grad_one = jnp.sum(grad_first * jnp.conj(probe_c), axis=0)
        patch = jnp.stack([grad_one, grad_second])
        current = lax.dynamic_slice(carry, (zero_index, row_start, col_start), (SLICES, WIN, WIN))
        carry = lax.dynamic_update_slice(carry, current + patch, (zero_index, row_start, col_start))
        return carry, None

    initial = jnp.zeros(padded.shape, dtype=padded.dtype)
    total, _ = lax.scan(advance, initial, (start_rows, start_cols, measured_flat))
    inside = total[:, :NR, :NC]
    return jnp.stack([jnp.real(inside), jnp.imag(inside)], axis=1).astype(objects.dtype)
```

```python
import math, functools
import numpy as np
import jax, jax.numpy as jnp
from jax import lax
from jax.experimental import pallas as pl
from jax.sharding import PartitionSpec as P
from jax.experimental.pallas import tpu as pltpu
F32=jnp.float32; BF16=jnp.bfloat16

def tables(n):
    k=np.arange(n); ang=(k[:,None]*k[None,:]%n)*(2*math.pi/n); f=1/math.sqrt(n)
    c=np.cos(ang)*f; s=np.sin(ang)*f
    fwd=np.block([[c,-s],[s,c]])
    inv=fwd.T
    def split(m):
        hi=m.astype(jnp.bfloat16); lo=(m-hi.astype(np.float64)).astype(jnp.bfloat16); return hi,lo
    fh,fl=split(fwd); ih,il=split(inv)
    right=np.stack([np.concatenate([fh,fh,fl],0),np.concatenate([ih,ih,il],0)])
    left=np.stack([np.concatenate([ih,ih,il],1),np.concatenate([fh,fh,fl],1)])
    return jnp.asarray(right),jnp.asarray(left)

def split(x):
    hi=x.astype(BF16)
    return hi,(x-hi.astype(F32)).astype(BF16)

def fourier(fields, way, right, left):
    n=fields[0][0][0].shape[0]; modes=len(fields[0])
    x=jnp.concatenate([jnp.concatenate(f,1) for pos in fields for f in pos],0)
    hi,lo=split(x)
    y=jnp.dot(jnp.concatenate([hi,lo,hi],1),right[way],preferred_element_type=F32)
    cols=[]
    for p in range(len(fields)):
        for m in range(modes):
            b=y[(p*modes+m)*n:(p*modes+m+1)*n]
            cols.append(jnp.concatenate([b[:,:n],b[:,n:]],0))
    y=jnp.concatenate(cols,1)
    hi,lo=split(y)
    z=jnp.dot(left[way],jnp.concatenate([hi,lo,hi],0),preferred_element_type=F32)
    out=[]
    for p in range(len(fields)):
        row=[]
        for m in range(modes):
            i=p*modes+m
            row.append((z[:n,i*n:(i+1)*n],z[n:,i*n:(i+1)*n]))
        out.append(row)
    return out

def cmul(a,b): return a[0]*b[0]-a[1]*b[1], a[0]*b[1]+a[1]*b[0]
def cmulc(a,b): return a[0]*b[0]+a[1]*b[1], a[1]*b[0]-a[0]*b[1]

def take(ref, lead, r, c, n):
    lanes=n
    cb=pl.multiple_of((c//n)*n,n); cs=c%n; rb=pl.multiple_of((r//8)*8,8); rs=r%8
    g=n//8
    lane=lax.broadcasted_iota(jnp.int32,(g+1,8,n),2)
    sub=lax.broadcasted_iota(jnp.int32,(g,8,n),1)
    v=ref[lead+(pl.ds(rb,n+8),pl.ds(cb,2*n))]
    v0=v[:,:n].reshape(g+1,8,n); v1=v[:,n:].reshape(g+1,8,n)
    sh=(n-cs)%n
    w=jnp.where(lane<n-cs,pltpu.roll(v0,sh,2),pltpu.roll(v1,sh,2))
    w=pltpu.roll(w,(8-rs)%8,1)
    return jnp.where(sub<8-rs,w[:g],w[1:]).reshape(n,n)

def put(ref, lead, r, c, val):
    n=val.shape[0]; g=n//8
    cb=pl.multiple_of((c//n)*n,n); cs=c%n; rb=pl.multiple_of((r//8)*8,8); rs=r%8
    lane=lax.broadcasted_iota(jnp.int32,(g+1,8,n),2)
    sub=lax.broadcasted_iota(jnp.int32,(g+1,8,n),1)
    w=pltpu.roll(val.reshape(g,8,n),rs,1)
    z=jnp.zeros((1,8,n),F32)
    w=jnp.where(sub>=rs,jnp.concatenate([w,z],0),jnp.concatenate([z,w],0))
    w=pltpu.roll(w,cs,2)
    zz=jnp.zeros_like(w)
    a=jnp.where(lane>=cs,w,zz).reshape(n+8,n); b=jnp.where(lane<cs,w,zz).reshape(n+8,n)
    ref[lead+(pl.ds(rb,n+8),pl.ds(cb,2*n))]+=jnp.concatenate([a,b],1)

def kernel(U, off, tile, right, lower, corner, prob, other, prop, meas, rt, lt, own, gr, gl, gc, ext, acc):
    n=prob.shape[-1]; t=tile.shape[-1]
    ext[:,:,:t,:t]=tile[...]; ext[:,:,:t,t:]=right[...]; ext[:,:,t:,:t]=lower[...]; ext[:,:,t:,t:]=corner[...]
    acc[...]=jnp.zeros_like(acc)
    modes=[(prob[0],prob[1]),(other[0],other[1])]
    H=(prop[0],prop[1]); Hc=(prop[0],-prop[1])
    def body(i,_):
        ps=[i*U+u for u in range(U)]
        rc=[(off[p,0],off[p,1]) for p in ps]
        w1=[(take(ext,(0,0),r,c,n),take(ext,(0,1),r,c,n)) for r,c in rc]
        w2=[(take(ext,(1,0),r,c,n),take(ext,(1,1),r,c,n)) for r,c in rc]
        a=[[cmul(q,w) for q in modes] for w in w1]
        a=fourier(a,0,rt,lt)
        a=[[cmul(f,H) for f in row] for row in a]
        b=fourier(a,1,rt,lt)
        f=[[cmul(x,w) for x in row] for row,w in zip(b,w2)]
        f=fourier(f,0,rt,lt)
        g=[]
        for p,row in zip(ps,f):
            res=4.0*(row[0][0]**2+row[0][1]**2+(row[1][0]**2+row[1][1]**2)-meas[p])
            g.append([(res*x,res*y) for x,y in row])
        g=fourier(g,1,rt,lt)
        for (r,c),gp,bp in zip(rc,g,b):
            s=[cmulc(x,y) for x,y in zip(gp,bp)]
            put(acc,(1,0),r,c,s[0][0]+s[1][0]); put(acc,(1,1),r,c,s[0][1]+s[1][1])
        g=[[cmulc(x,w) for x in row] for row,w in zip(g,w2)]
        g=fourier(g,0,rt,lt)
        g=[[cmulc(x,H) for x in row] for row in g]
        g=fourier(g,1,rt,lt)
        for (r,c),gp in zip(rc,g):
            s=[cmulc(x,y) for x,y in zip(gp,modes)]
            put(acc,(0,0),r,c,s[0][0]+s[1][0]); put(acc,(0,1),r,c,s[0][1]+s[1][1])
        return 0
    lax.fori_loop(0,off.shape[0]//U,body,0)
    own[...]=acc[:,:,:t,:t]; gr[...]=acc[:,:,:t,t:]; gl[...]=acc[:,:,t:,:t]; gc[...]=acc[:,:,t:,t:]

def call(U,off,tile,right,lower,corner,prob,other,prop,meas,rt,lt):
    n=prob.shape[-1]; t=tile.shape[-1]; s=tile.shape[0]
    V=pl.BlockSpec(memory_space=pltpu.VMEM)
    sd=lambda *x: jax.ShapeDtypeStruct(x,F32)
    return pl.pallas_call(functools.partial(kernel,U),
      out_shape=(sd(s,2,t,t),sd(s,2,t,n),sd(s,2,n,t),sd(s,2,n,n)),
      in_specs=[pl.BlockSpec(memory_space=pltpu.SMEM)]+[V]*10,
      scratch_shapes=[pltpu.VMEM((s,2,t+n,t+n),F32)]*2,
      compiler_params=pltpu.CompilerParams(vmem_limit_bytes=48<<20),
      )(off,tile,right,lower,corner,prob,other,prop,meas,rt,lt)


def passed_along(value, axis, by):
    count = lax.axis_size(axis)
    pairs = [(i, i + by) for i in range(count) if 0 <= i + by < count]
    return lax.ppermute(value, axis, pairs)


def passed_across(value, by):
    rows, cols = lax.axis_size("row"), lax.axis_size("col")
    pairs = [
        (r * cols + c, (r + by) * cols + c + by)
        for r in range(rows)
        for c in range(cols)
        if 0 <= r + by < rows and 0 <= c + by < cols
    ]
    return lax.ppermute(value, ("row", "col"), pairs)


def combine(own, right, lower, corner, out):
    n = corner.shape[-1]
    out[...] = own[...]
    out[:, :, :, :n] += right[...]
    out[:, :, :n, :] += lower[...]
    out[:, :, :n, :n] += corner[...]


def on_device(objects, probes, phase, offsets, measured):
    n = probes.shape[2]
    lower = passed_along(objects[:, :, :n, :], "row", -1)
    corner = passed_across(objects[:, :, :n, :n], -1)
    right = passed_along(objects[:, :, :, :n], "col", -1)
    other = lax.ppermute(probes, "mode", [(0, 1), (1, 0)])
    prop = jnp.stack([jnp.cos(phase), jnp.sin(phase)])
    rt, lt = tables(n)
    own, gr, gl, gc = call(4, offsets[0, 0], objects, right, lower, corner, probes[0], other[0], prop, measured[0, 0], rt, lt)
    gl = passed_along(gl, "row", 1)
    gc = passed_across(gc, 1)
    gr = passed_along(gr, "col", 1)
    V = pl.BlockSpec(memory_space=pltpu.VMEM)
    return pl.pallas_call(
        combine,
        out_shape=jax.ShapeDtypeStruct(objects.shape, jnp.float32),
        in_specs=[V] * 4,
        out_specs=V,
        compiler_params=pltpu.CompilerParams(vmem_limit_bytes=24 << 20),
    )(own, gr, gl, gc)


def solution(mesh):
    placed = (
        P(None, None, "row", "col"),
        P("mode", None, None, None),
        P(),
        P("row", "col", None, None),
        P("row", "col", None, None, None),
    )
    return jax.shard_map(
        on_device,
        mesh=mesh,
        in_specs=placed,
        out_specs=P(None, None, "row", "col"),
        check_vma=False,
    )
```

```python
import functools
import math

import jax
import jax.numpy as jnp
import numpy as np
from jax import lax
from jax.experimental import pallas as pl
from jax.experimental.pallas import tpu as pltpu
from jax.sharding import PartitionSpec as P

F32 = jnp.float32
BF16 = jnp.bfloat16
FORWARD, INVERSE = 0, 1
GROUP = 4
VMEM = pl.BlockSpec(memory_space=pltpu.VMEM)
SMEM = pl.BlockSpec(memory_space=pltpu.SMEM)


def passed_along(value, axis, by):
    count = lax.axis_size(axis)
    pairs = [(i, i + by) for i in range(count) if 0 <= i + by < count]
    return lax.ppermute(value, axis, pairs)


def passed_across(value, by):
    rows, cols = lax.axis_size("row"), lax.axis_size("col")
    pairs = [
        (r * cols + c, (r + by) * cols + c + by)
        for r in range(rows)
        for c in range(cols)
        if 0 <= r + by < rows and 0 <= c + by < cols
    ]
    return lax.ppermute(value, ("row", "col"), pairs)


def tables(length):
    counter = np.arange(length)
    angle = (counter[:, None] * counter[None, :] % length) * (2.0 * math.pi / length)
    cos, sin = np.cos(angle) / math.sqrt(length), np.sin(angle) / math.sqrt(length)
    forward = np.block([[cos, -sin], [sin, cos]])
    kept = []
    for table in (forward, forward.T):
        high = table.astype(jnp.bfloat16)
        kept.append(np.stack([high, (table - high.astype(np.float64)).astype(jnp.bfloat16)]))
    return jnp.asarray(np.stack(kept))


def parts(value):
    high = value.astype(BF16)
    return high, (value - high.astype(F32)).astype(BF16)


def fourier(modes, way, table):
    n = modes[0][0].shape[0]
    right_high, right_low = table[way, 0], table[way, 1]
    left_high, left_low = table[1 - way, 0], table[1 - way, 1]
    high, low = parts(jnp.concatenate([jnp.concatenate(pair, 1) for pair in modes], 0))
    rows = jnp.dot(
        jnp.concatenate([high, low, high], 1),
        jnp.concatenate([right_high, right_high, right_low], 0),
        preferred_element_type=F32,
    )
    stacked = [
        jnp.concatenate([rows[i * n : (i + 1) * n, :n], rows[i * n : (i + 1) * n, n:]], 0) for i in range(len(modes))
    ]
    high, low = parts(jnp.concatenate(stacked, 1))
    both = jnp.dot(
        jnp.concatenate([left_high, left_high, left_low], 1),
        jnp.concatenate([high, low, high], 0),
        preferred_element_type=F32,
    )
    return [(both[:n, i * n : (i + 1) * n], both[n:, i * n : (i + 1) * n]) for i in range(len(modes))]


def times(a, b):
    return a[0] * b[0] - a[1] * b[1], a[0] * b[1] + a[1] * b[0]


def times_conj(a, b):
    return a[0] * b[0] + a[1] * b[1], a[1] * b[0] - a[0] * b[1]


def summed(values):
    return functools.reduce(lambda a, b: a + b, values)


def place_of(offsets, position, n):
    row, col = offsets[position, 0], offsets[position, 1]
    rows = pl.ds(pl.multiple_of(row // 8 * 8, 8), n + 8)
    cols = pl.ds(pl.multiple_of(col // n * n, n), 2 * n)
    return rows, cols, row % 8, col % n


def cut(source, channel, place, n):
    rows, cols, down, across = place
    groups = n // 8
    lane = lax.broadcasted_iota(jnp.int32, (groups + 1, 8, n), 2)
    line = lax.broadcasted_iota(jnp.int32, (groups, 8, n), 1)
    wide = source[channel, rows, cols]
    turn = (n - across) % n
    first = pltpu.roll(wide[:, :n].reshape(groups + 1, 8, n), turn, 2)
    second = pltpu.roll(wide[:, n:].reshape(groups + 1, 8, n), turn, 2)
    tall = pltpu.roll(jnp.where(lane < n - across, first, second), (8 - down) % 8, 1)
    return jnp.where(line < 8 - down, tall[:groups], tall[1:]).reshape(n, n)


def deposit(target, channel, place, value):
    rows, cols, down, across = place
    n = value.shape[0]
    groups = n // 8
    lane = lax.broadcasted_iota(jnp.int32, (groups + 1, 8, n), 2)
    line = lax.broadcasted_iota(jnp.int32, (groups + 1, 8, n), 1)
    turned = pltpu.roll(value.reshape(groups, 8, n), down, 1)
    blank = jnp.zeros((1, 8, n), F32)
    tall = jnp.where(line >= down, jnp.concatenate([turned, blank], 0), jnp.concatenate([blank, turned], 0))
    tall = pltpu.roll(tall, across, 2)
    zero = jnp.zeros_like(tall)
    first = jnp.where(lane >= across, tall, zero).reshape(n + 8, n)
    second = jnp.where(lane < across, tall, zero).reshape(n + 8, n)
    target[channel, rows, cols] += jnp.concatenate([first, second], 1)


def cut_pair(source, place, n):
    return cut(source, 0, place, n), cut(source, 1, place, n)


def deposit_pair(target, place, terms):
    for channel in range(2):
        deposit(target, channel, place, summed([term[channel] for term in terms]))


def keep(target, position, modes):
    for m, (re, im) in enumerate(modes):
        target[position, m, 0] = re
        target[position, m, 1] = im


def kept(source, position):
    return [(source[position, m, 0], source[position, m, 1]) for m in range(source.shape[1])]


def groups_of(count):
    return [range(k, min(k + GROUP, count)) for k in range(0, count, GROUP)]


def join(extended, tile, right, lower, corner):
    t = tile.shape[-1]
    extended[:, :t, :t] = tile[...]
    extended[:, :t, t:] = right[...]
    extended[:, t:, :t] = lower[...]
    extended[:, t:, t:] = corner[...]


def part_ways(total, own, right, lower, corner):
    t = own.shape[-1]
    own[...] = total[:, :t, :t]
    right[...] = total[:, :t, t:]
    lower[...] = total[:, t:, :t]
    corner[...] = total[:, t:, t:]


def pack_kernel(objects, tile, lower0, corner, right0):
    n = corner.shape[-1]
    lower0[...] = objects[0, :, :n, :]
    corner[...] = objects[:, :, :n, :n]
    right0[...] = objects[0, :, :, :n]
    tile[...] = objects[...]


def stage_kernel(tile, table, lower1, right1, table_out):
    n = right1.shape[-1]
    lower1[...] = tile[1, :, :n, :]
    right1[...] = tile[1, :, :, :n]
    table_out[...] = table[...]


def factor_kernel(*refs):
    phase, out = refs[-2:]
    for m, probe in enumerate(refs[:-2]):
        out[m] = probe[...]
    out[len(refs) - 2, 0] = jnp.cos(phase[...])
    out[len(refs) - 2, 1] = jnp.sin(phase[...])


def factors_of(factors):
    pairs = [(factors[m, 0], factors[m, 1]) for m in range(factors.shape[0])]
    return pairs[:-1], pairs[-1]


def middle_kernel(offsets, objects, right, lower, corner, factors, table, middle, extended):
    n = corner.shape[-1]
    join(extended, objects.at[0], right, lower, corner.at[0])
    probes, spread = factors_of(factors)
    for group in groups_of(offsets.shape[0]):
        windows = [cut_pair(extended, place_of(offsets, k, n), n) for k in group]
        waves = [[times(p, window) for p in probes] for window in windows]
        waves = [fourier(wave, FORWARD, table) for wave in waves]
        waves = [[times(w, spread) for w in wave] for wave in waves]
        waves = [fourier(wave, INVERSE, table) for wave in waves]
        for k, wave in zip(group, waves):
            keep(middle, k, wave)


def second_kernel(
    offsets, objects, right, lower, corner, middle, measured, table,
    back, own, rim_right, rim_lower, rim_corner, extended, total,
):
    n = corner.shape[-1]
    join(extended, objects.at[1], right, lower, corner.at[1])
    total[...] = jnp.zeros_like(total)
    for group in groups_of(offsets.shape[0]):
        windows = [cut_pair(extended, place_of(offsets, k, n), n) for k in group]
        waves = [kept(middle, k) for k in group]
        far = [[times(w, window) for w in wave] for wave, window in zip(waves, windows)]
        far = [fourier(wave, FORWARD, table) for wave in far]
        grads = []
        for k, wave in zip(group, far):
            resid = 4.0 * (summed([re * re + im * im for re, im in wave]) - measured[k])
            grads.append([(resid * re, resid * im) for re, im in wave])
        grads = [fourier(grad, INVERSE, table) for grad in grads]
        for k, grad, window in zip(group, grads, windows):
            keep(back, k, [times_conj(g, window) for g in grad])
        for k, grad, wave in zip(group, grads, waves):
            deposit_pair(total, place_of(offsets, k, n), [times_conj(g, w) for g, w in zip(grad, wave)])
    part_ways(total, own, rim_right, rim_lower, rim_corner)


def first_kernel(
    offsets, back, factors, table, other_right, other_corner, own, rim_right, rim_lower, rim_corner, total
):
    n = rim_corner.shape[-1]
    probes, spread = factors_of(factors)
    total[...] = jnp.zeros_like(total)
    rim_right[1] = other_right[...]
    rim_corner[1] = other_corner[...]
    for group in groups_of(offsets.shape[0]):
        waves = [fourier(kept(back, k), FORWARD, table) for k in group]
        waves = [[times_conj(w, spread) for w in wave] for wave in waves]
        waves = [fourier(wave, INVERSE, table) for wave in waves]
        for k, wave in zip(group, waves):
            deposit_pair(total, place_of(offsets, k, n), [times_conj(w, p) for w, p in zip(wave, probes)])
    part_ways(total, own, rim_right.at[0], rim_lower, rim_corner.at[0])


def add_lower_kernel(own, lower, out):
    n = lower.shape[-2]
    out[:, n:] = own[:, n:]
    out[:, :n] = own[:, :n] + lower[...]


def combine_kernel(own0, own1, right, lower0, corner, out):
    n = corner.shape[-1]
    out[0] = own0[...]
    out[1] = own1[...]
    out[0, :, :n, :] += lower0[...]
    for s in range(out.shape[0]):
        out[s, :, :, :n] += right[s]
        out[s, :, :n, :n] += corner[s]


def cost(transforms, n):
    return pl.CostEstimate(flops=transforms * 24 * n * n * n, bytes_accessed=1 << 22, transcendentals=0)


def on_device(objects, probes, phase, offsets, measured):
    slices, _, t, _ = objects.shape
    n = probes.shape[2]
    reach = t + n
    mode_count = lax.axis_size("mode")
    starts, targets = offsets[0, 0], measured[0, 0]
    count = starts.shape[0]
    shape = lambda *dims: jax.ShapeDtypeStruct(dims, F32)
    params = pltpu.CompilerParams(vmem_limit_bytes=40 << 20)
    rim_right, rim_lower, rim_corner = shape(slices, 2, t, n), shape(2, n, t), shape(slices, 2, n, n)

    tile, lower0, corner, right0 = pl.pallas_call(
        pack_kernel,
        out_shape=(shape(*objects.shape), rim_lower, rim_corner, shape(2, t, n)),
        in_specs=[VMEM],
        out_specs=(VMEM,) * 4,
        compiler_params=params,
    )(objects)
    lower0 = passed_along(lower0, "row", -1)
    corner = passed_across(corner, -1)
    right0 = passed_along(right0, "col", -1)
    received = []
    for by in range(1, mode_count):
        received.append(lax.ppermute(probes, "mode", [(i, (i + by) % mode_count) for i in range(mode_count)])[0])

    table = tables(n)
    lower1, right1, table = pl.pallas_call(
        stage_kernel,
        out_shape=(rim_lower, shape(2, t, n), jax.ShapeDtypeStruct(table.shape, table.dtype)),
        in_specs=[VMEM] * 2,
        out_specs=(VMEM,) * 3,
        compiler_params=params,
    )(tile, table)
    lower1 = passed_along(lower1, "row", -1)
    right1 = passed_along(right1, "col", -1)
    factors = pl.pallas_call(
        factor_kernel,
        out_shape=shape(mode_count + 1, 2, n, n),
        in_specs=[VMEM] * (mode_count + 1),
        out_specs=VMEM,
        compiler_params=params,
    )(probes[0], *received, phase)
    waves = shape(count, mode_count, 2, n, n)
    window_area = pltpu.VMEM((2, reach, reach), F32)
    middle = pl.pallas_call(
        middle_kernel,
        out_shape=waves,
        in_specs=[SMEM] + [VMEM] * 6,
        out_specs=VMEM,
        scratch_shapes=[window_area],
        compiler_params=params,
        cost_estimate=cost(12 * count * mode_count, n),
    )(starts, tile, right0, lower0, corner, factors, table)

    back, own1, grad_right, grad_lower1, grad_corner = pl.pallas_call(
        second_kernel,
        out_shape=(waves, shape(2, t, t), shape(2, t, n), rim_lower, shape(2, n, n)),
        in_specs=[SMEM] + [VMEM] * 7,
        out_specs=(VMEM,) * 5,
        scratch_shapes=[window_area] * 2,
        compiler_params=params,
        cost_estimate=cost(6 * count * mode_count, n),
    )(starts, tile, right1, lower1, corner, middle, targets, table)
    grad_lower1 = passed_along(grad_lower1, "row", 1)

    own0, grad_right, grad_lower0, grad_corner = pl.pallas_call(
        first_kernel,
        out_shape=(shape(2, t, t), rim_right, rim_lower, rim_corner),
        in_specs=[SMEM] + [VMEM] * 5,
        out_specs=(VMEM,) * 4,
        scratch_shapes=[window_area],
        compiler_params=params,
        cost_estimate=cost(6 * count * mode_count, n),
    )(starts, back, factors, table, grad_right, grad_corner)
    grad_lower0 = passed_along(grad_lower0, "row", 1)
    grad_right = passed_along(grad_right, "col", 1)
    grad_corner = passed_across(grad_corner, 1)

    own1 = pl.pallas_call(
        add_lower_kernel,
        out_shape=shape(2, t, t),
        in_specs=[VMEM] * 2,
        out_specs=VMEM,
        input_output_aliases={0: 0},
        compiler_params=params,
        cost_estimate=cost(64, n),
    )(own1, grad_lower1)
    return pl.pallas_call(
        combine_kernel,
        out_shape=jax.ShapeDtypeStruct(objects.shape, F32),
        in_specs=[VMEM] * 5,
        out_specs=VMEM,
        compiler_params=params,
    )(own0, own1, grad_right, grad_lower0, grad_corner)


def solution(mesh):
    placed = (
        P(None, None, "row", "col"),
        P("mode", None, None, None),
        P(),
        P("row", "col", None, None),
        P("row", "col", None, None, None),
    )
    return jax.shard_map(
        on_device,
        mesh=mesh,
        in_specs=placed,
        out_specs=P(None, None, "row", "col"),
        check_vma=False,
    )
```

```python
import functools
import math

import jax
import jax.numpy as jnp
import numpy as np
from jax import lax
from jax.experimental import pallas as pl
from jax.experimental.pallas import tpu as pltpu
from jax.sharding import PartitionSpec as P

F32 = jnp.float32
BF16 = jnp.bfloat16
FORWARD, INVERSE = 0, 1
GROUP = 4
VMEM = pl.BlockSpec(memory_space=pltpu.VMEM)
SMEM = pl.BlockSpec(memory_space=pltpu.SMEM)


def passed_along(value, axis, by):
    count = lax.axis_size(axis)
    pairs = [(i, i + by) for i in range(count) if 0 <= i + by < count]
    return lax.ppermute(value, axis, pairs)


def passed_across(value, by):
    rows, cols = lax.axis_size("row"), lax.axis_size("col")
    pairs = [
        (r * cols + c, (r + by) * cols + c + by)
        for r in range(rows)
        for c in range(cols)
        if 0 <= r + by < rows and 0 <= c + by < cols
    ]
    return lax.ppermute(value, ("row", "col"), pairs)


def tables(length):
    counter = np.arange(length)
    angle = (counter[:, None] * counter[None, :] % length) * (2.0 * math.pi / length)
    cos, sin = np.cos(angle) / math.sqrt(length), np.sin(angle) / math.sqrt(length)
    forward = np.block([[cos, -sin], [sin, cos]])
    kept = []
    for table in (forward, forward.T):
        high = table.astype(jnp.bfloat16)
        kept.append(np.stack([high, (table - high.astype(np.float64)).astype(jnp.bfloat16)]))
    return jnp.asarray(np.stack(kept))


def parts(value):
    high = value.astype(BF16)
    return high, (value - high.astype(F32)).astype(BF16)


def fourier(modes, way, table):
    n = modes[0][0].shape[0]
    right_high, right_low = table[way, 0], table[way, 1]
    left_high, left_low = table[1 - way, 0], table[1 - way, 1]
    high, low = parts(jnp.concatenate([jnp.concatenate(pair, 1) for pair in modes], 0))
    rows = jnp.dot(
        jnp.concatenate([high, low, high], 1),
        jnp.concatenate([right_high, right_high, right_low], 0),
        preferred_element_type=F32,
    )
    stacked = [
        jnp.concatenate([rows[i * n : (i + 1) * n, :n], rows[i * n : (i + 1) * n, n:]], 0) for i in range(len(modes))
    ]
    high, low = parts(jnp.concatenate(stacked, 1))
    both = jnp.dot(
        jnp.concatenate([left_high, left_high, left_low], 1),
        jnp.concatenate([high, low, high], 0),
        preferred_element_type=F32,
    )
    return [(both[:n, i * n : (i + 1) * n], both[n:, i * n : (i + 1) * n]) for i in range(len(modes))]


def times(a, b):
    return a[0] * b[0] - a[1] * b[1], a[0] * b[1] + a[1] * b[0]


def times_conj(a, b):
    return a[0] * b[0] + a[1] * b[1], a[1] * b[0] - a[0] * b[1]


def summed(values):
    return functools.reduce(lambda a, b: a + b, values)


def place_of(offsets, position, n):
    row, col = offsets[position, 0], offsets[position, 1]
    rows = pl.ds(pl.multiple_of(row // 8 * 8, 8), n + 8)
    cols = pl.ds(pl.multiple_of(col // n * n, n), 2 * n)
    return rows, cols, row % 8, col % n


def cut(source, channel, place, n):
    rows, cols, down, across = place
    groups = n // 8
    lane = lax.broadcasted_iota(jnp.int32, (groups + 1, 8, n), 2)
    line = lax.broadcasted_iota(jnp.int32, (groups, 8, n), 1)
    wide = source[channel, rows, cols]
    turn = (n - across) % n
    first = pltpu.roll(wide[:, :n].reshape(groups + 1, 8, n), turn, 2)
    second = pltpu.roll(wide[:, n:].reshape(groups + 1, 8, n), turn, 2)
    tall = pltpu.roll(jnp.where(lane < n - across, first, second), (8 - down) % 8, 1)
    return jnp.where(line < 8 - down, tall[:groups], tall[1:]).reshape(n, n)


def deposit(target, channel, place, value):
    rows, cols, down, across = place
    n = value.shape[0]
    groups = n // 8
    lane = lax.broadcasted_iota(jnp.int32, (groups + 1, 8, n), 2)
    line = lax.broadcasted_iota(jnp.int32, (groups + 1, 8, n), 1)
    turned = pltpu.roll(value.reshape(groups, 8, n), down, 1)
    blank = jnp.zeros((1, 8, n), F32)
    tall = jnp.where(line >= down, jnp.concatenate([turned, blank], 0), jnp.concatenate([blank, turned], 0))
    tall = pltpu.roll(tall, across, 2)
    zero = jnp.zeros_like(tall)
    first = jnp.where(lane >= across, tall, zero).reshape(n + 8, n)
    second = jnp.where(lane < across, tall, zero).reshape(n + 8, n)
    target[channel, rows, cols] += jnp.concatenate([first, second], 1)


def cut_pair(source, place, n):
    return cut(source, 0, place, n), cut(source, 1, place, n)


def deposit_pair(target, place, terms):
    for channel in range(2):
        deposit(target, channel, place, summed([term[channel] for term in terms]))


def keep(target, position, modes):
    for m, (re, im) in enumerate(modes):
        target[position, m, 0] = re
        target[position, m, 1] = im


def kept(source, position):
    return [(source[position, m, 0], source[position, m, 1]) for m in range(source.shape[1])]


def groups_of(count):
    return [range(k, min(k + GROUP, count)) for k in range(0, count, GROUP)]


def join(extended, tile, right, lower, corner):
    t = tile.shape[-1]
    extended[:, :t, :t] = tile[...]
    extended[:, :t, t:] = right[...]
    extended[:, t:, :t] = lower[...]
    extended[:, t:, t:] = corner[...]


def part_ways(total, own, right, lower, corner):
    t = own.shape[-1]
    own[...] = total[:, :t, :t]
    right[...] = total[:, :t, t:]
    lower[...] = total[:, t:, :t]
    corner[...] = total[:, t:, t:]


def pack_kernel(objects, tile, lower0, corner, right0, sems):
    n = corner.shape[-1]
    pieces = (
        (objects.at[:, :, pl.ds(0, n), pl.ds(0, n)], corner),
        (objects.at[0, :, pl.ds(0, n), :], lower0),
        (objects.at[0, :, :, pl.ds(0, n)], right0),
        (objects, tile),
    )
    copies = [pltpu.make_async_copy(piece, out, sems.at[i]) for i, (piece, out) in enumerate(pieces)]
    for copy in copies:
        copy.start()
    for copy in copies:
        copy.wait()


def stage_kernel(tile, lower1):
    lower1[...] = tile[1, :, : lower1.shape[-2], :]


def factor_kernel(*refs):
    tile, phase, table, out, table_out, right1 = refs[-6:]
    probes = refs[:-6]
    for m, probe in enumerate(probes):
        out[m] = probe[...]
    out[len(probes), 0] = jnp.cos(phase[...])
    out[len(probes), 1] = jnp.sin(phase[...])
    table_out[...] = table[...]
    right1[...] = tile[1, :, :, : right1.shape[-1]]


def factors_of(factors):
    pairs = [(factors[m, 0], factors[m, 1]) for m in range(factors.shape[0])]
    return pairs[:-1], pairs[-1]


def middle_kernel(offsets, objects, right, lower, corner, factors, table, middle, extended):
    n = corner.shape[-1]
    join(extended, objects.at[0], right, lower, corner.at[0])
    probes, spread = factors_of(factors)
    for group in groups_of(offsets.shape[0]):
        windows = [cut_pair(extended, place_of(offsets, k, n), n) for k in group]
        waves = [[times(p, window) for p in probes] for window in windows]
        waves = [fourier(wave, FORWARD, table) for wave in waves]
        waves = [[times(w, spread) for w in wave] for wave in waves]
        waves = [fourier(wave, INVERSE, table) for wave in waves]
        for k, wave in zip(group, waves):
            keep(middle, k, wave)


def second_kernel(
    offsets, objects, right, lower, corner, middle, measured, table,
    back, own, rim_right, rim_lower, rim_corner, extended, total,
):
    n = corner.shape[-1]
    join(extended, objects.at[1], right, lower, corner.at[1])
    total[...] = jnp.zeros_like(total)
    for group in groups_of(offsets.shape[0]):
        windows = [cut_pair(extended, place_of(offsets, k, n), n) for k in group]
        waves = [kept(middle, k) for k in group]
        far = [[times(w, window) for w in wave] for wave, window in zip(waves, windows)]
        far = [fourier(wave, FORWARD, table) for wave in far]
        grads = []
        for k, wave in zip(group, far):
            resid = 4.0 * (summed([re * re + im * im for re, im in wave]) - measured[k])
            grads.append([(resid * re, resid * im) for re, im in wave])
        grads = [fourier(grad, INVERSE, table) for grad in grads]
        for k, grad, window in zip(group, grads, windows):
            keep(back, k, [times_conj(g, window) for g in grad])
        for k, grad, wave in zip(group, grads, waves):
            deposit_pair(total, place_of(offsets, k, n), [times_conj(g, w) for g, w in zip(grad, wave)])
    part_ways(total, own, rim_right, rim_lower, rim_corner)


def first_kernel(
    offsets, back, factors, table, other_right, other_corner, own, rim_right, rim_lower, rim_corner, total
):
    n = rim_corner.shape[-1]
    probes, spread = factors_of(factors)
    total[...] = jnp.zeros_like(total)
    rim_right[1] = other_right[...]
    rim_corner[1] = other_corner[...]
    for group in groups_of(offsets.shape[0]):
        waves = [fourier(kept(back, k), FORWARD, table) for k in group]
        waves = [[times_conj(w, spread) for w in wave] for wave in waves]
        waves = [fourier(wave, INVERSE, table) for wave in waves]
        for k, wave in zip(group, waves):
            deposit_pair(total, place_of(offsets, k, n), [times_conj(w, p) for w, p in zip(wave, probes)])
    part_ways(total, own, rim_right.at[0], rim_lower, rim_corner.at[0])


def add_lower_kernel(own, lower, out):
    n = lower.shape[-2]
    out[:, n:] = own[:, n:]
    out[:, :n] = own[:, :n] + lower[...]


def add_right_kernel(own0, own1, right, out):
    n = right.shape[-1]
    for s, own in enumerate((own0, own1)):
        out[s, :, :, n:] = own[:, :, n:]
        out[s, :, :, :n] = own[:, :, :n] + right[s]


def add_corner_kernel(own, corner, out):
    n = corner.shape[-1]
    out[...] = own[...]
    out[:, :, :n, :n] += corner[...]


def cost(transforms, n):
    return pl.CostEstimate(flops=transforms * 24 * n * n * n, bytes_accessed=1 << 22, transcendentals=0)


def on_device(objects, probes, phase, offsets, measured):
    slices, _, t, _ = objects.shape
    n = probes.shape[2]
    reach = t + n
    mode_count = lax.axis_size("mode")
    starts, targets = offsets[0, 0], measured[0, 0]
    count = starts.shape[0]
    shape = lambda *dims: jax.ShapeDtypeStruct(dims, F32)
    params = pltpu.CompilerParams(vmem_limit_bytes=24 << 20)
    small = pltpu.CompilerParams(vmem_limit_bytes=8 << 20)
    rim_right, rim_lower, rim_corner = shape(slices, 2, t, n), shape(2, n, t), shape(slices, 2, n, n)

    tile, lower0, corner, right0 = pl.pallas_call(
        pack_kernel,
        out_shape=(shape(*objects.shape), rim_lower, rim_corner, shape(2, t, n)),
        in_specs=[pl.BlockSpec(memory_space=pltpu.HBM)],
        out_specs=(VMEM,) * 4,
        scratch_shapes=[pltpu.SemaphoreType.DMA((4,))],
        compiler_params=small,
    )(objects)
    lower0 = passed_along(lower0, "row", -1)
    corner = passed_across(corner, -1)
    right0 = passed_along(right0, "col", -1)
    received = []
    for by in range(1, mode_count):
        received.append(lax.ppermute(probes, "mode", [(i, (i + by) % mode_count) for i in range(mode_count)])[0])

    lower1 = pl.pallas_call(
        stage_kernel, out_shape=rim_lower, in_specs=[VMEM], out_specs=VMEM, compiler_params=small
    )(tile)
    lower1 = passed_along(lower1, "row", -1)
    table = tables(n)
    factors, table, right1 = pl.pallas_call(
        factor_kernel,
        out_shape=(
            shape(mode_count + 1, 2, n, n),
            jax.ShapeDtypeStruct(table.shape, table.dtype),
            shape(2, t, n),
        ),
        in_specs=[VMEM] * (mode_count + 3),
        out_specs=(VMEM,) * 3,
        compiler_params=small,
    )(probes[0], *received, tile, phase, table)
    right1 = passed_along(right1, "col", -1)
    waves = shape(count, mode_count, 2, n, n)
    window_area = pltpu.VMEM((2, reach, reach), F32)
    middle = pl.pallas_call(
        middle_kernel,
        out_shape=waves,
        in_specs=[SMEM] + [VMEM] * 6,
        out_specs=VMEM,
        scratch_shapes=[window_area],
        compiler_params=params,
        cost_estimate=cost(12 * count * mode_count, n),
    )(starts, tile, right0, lower0, corner, factors, table)

    back, own1, grad_right1, grad_lower1, grad_corner1 = pl.pallas_call(
        second_kernel,
        out_shape=(waves, shape(2, t, t), shape(2, t, n), rim_lower, shape(2, n, n)),
        in_specs=[SMEM] + [VMEM] * 7,
        out_specs=(VMEM,) * 5,
        scratch_shapes=[window_area] * 2,
        compiler_params=params,
        cost_estimate=cost(6 * count * mode_count, n),
    )(starts, tile, right1, lower1, corner, middle, targets, table)
    grad_lower1 = passed_along(grad_lower1, "row", 1)
    own0, grad_right, grad_lower0, grad_corner = pl.pallas_call(
        first_kernel,
        out_shape=(shape(2, t, t), rim_right, rim_lower, rim_corner),
        in_specs=[SMEM] + [VMEM] * 5,
        out_specs=(VMEM,) * 4,
        scratch_shapes=[window_area],
        compiler_params=params,
        cost_estimate=cost(6 * count * mode_count, n),
    )(starts, back, factors, table, grad_right1, grad_corner1)
    grad_lower0 = passed_along(grad_lower0, "row", 1)
    grad_right = passed_along(grad_right, "col", 1)
    grad_corner = passed_across(grad_corner, 1)

    def with_lower(own, lower, weight):
        return pl.pallas_call(
            add_lower_kernel,
            out_shape=shape(2, t, t),
            in_specs=[VMEM] * 2,
            out_specs=VMEM,
            input_output_aliases={0: 0},
            compiler_params=small,
            cost_estimate=cost(weight, n),
        )(own, lower)

    own1 = with_lower(own1, grad_lower1, 20)
    own0 = with_lower(own0, grad_lower0, 90)
    own = pl.pallas_call(
        add_right_kernel,
        out_shape=shape(*objects.shape),
        in_specs=[VMEM] * 3,
        out_specs=VMEM,
        compiler_params=small,
        cost_estimate=cost(0, n),
    )(own0, own1, grad_right)
    return pl.pallas_call(
        add_corner_kernel,
        out_shape=shape(*objects.shape),
        in_specs=[VMEM] * 2,
        out_specs=VMEM,
        compiler_params=small,
    )(own, grad_corner)


def solution(mesh):
    placed = (
        P(None, None, "row", "col"),
        P("mode", None, None, None),
        P(),
        P("row", "col", None, None),
        P("row", "col", None, None, None),
    )
    return jax.shard_map(
        on_device,
        mesh=mesh,
        in_specs=placed,
        out_specs=P(None, None, "row", "col"),
        check_vma=False,
    )
```

```python
import functools
import math

import jax
import jax.numpy as jnp
import numpy as np
from jax import lax
from jax.experimental import pallas as pl
from jax.experimental.pallas import tpu as pltpu
from jax.sharding import PartitionSpec as P

F32 = jnp.float32
BF16 = jnp.bfloat16
FORWARD, INVERSE = 0, 1
GROUP = 4
VMEM = pl.BlockSpec(memory_space=pltpu.VMEM)
SMEM = pl.BlockSpec(memory_space=pltpu.SMEM)


def passed_along(value, axis, by):
    count = lax.axis_size(axis)
    pairs = [(i, i + by) for i in range(count) if 0 <= i + by < count]
    return lax.ppermute(value, axis, pairs)


def passed_across(value, by):
    rows, cols = lax.axis_size("row"), lax.axis_size("col")
    pairs = [
        (r * cols + c, (r + by) * cols + c + by)
        for r in range(rows)
        for c in range(cols)
        if 0 <= r + by < rows and 0 <= c + by < cols
    ]
    return lax.ppermute(value, ("row", "col"), pairs)


def tables(length):
    counter = np.arange(length)
    angle = (counter[:, None] * counter[None, :] % length) * (2.0 * math.pi / length)
    cos, sin = np.cos(angle) / math.sqrt(length), np.sin(angle) / math.sqrt(length)
    forward = np.block([[cos, -sin], [sin, cos]])
    kept = []
    for table in (forward, forward.T):
        high = table.astype(jnp.bfloat16)
        kept.append(np.stack([high, (table - high.astype(np.float64)).astype(jnp.bfloat16)]))
    return jnp.asarray(np.stack(kept))


def parts(value):
    high = value.astype(BF16)
    return high, (value - high.astype(F32)).astype(BF16)


def fourier(modes, way, table):
    n = modes[0][0].shape[0]
    right_high, right_low = table[way, 0], table[way, 1]
    left_high, left_low = table[1 - way, 0], table[1 - way, 1]
    high, low = parts(jnp.concatenate([jnp.concatenate(pair, 1) for pair in modes], 0))
    rows = jnp.dot(
        jnp.concatenate([high, low, high], 1),
        jnp.concatenate([right_high, right_high, right_low], 0),
        preferred_element_type=F32,
    )
    stacked = [
        jnp.concatenate([rows[i * n : (i + 1) * n, :n], rows[i * n : (i + 1) * n, n:]], 0) for i in range(len(modes))
    ]
    high, low = parts(jnp.concatenate(stacked, 1))
    both = jnp.dot(
        jnp.concatenate([left_high, left_high, left_low], 1),
        jnp.concatenate([high, low, high], 0),
        preferred_element_type=F32,
    )
    return [(both[:n, i * n : (i + 1) * n], both[n:, i * n : (i + 1) * n]) for i in range(len(modes))]


def times(a, b):
    return a[0] * b[0] - a[1] * b[1], a[0] * b[1] + a[1] * b[0]


def times_conj(a, b):
    return a[0] * b[0] + a[1] * b[1], a[1] * b[0] - a[0] * b[1]


def summed(values):
    return functools.reduce(lambda a, b: a + b, values)


def place_of(offsets, position, n):
    row, col = offsets[position, 0], offsets[position, 1]
    rows = pl.ds(pl.multiple_of(row // 8 * 8, 8), n + 8)
    cols = pl.ds(pl.multiple_of(col // n * n, n), 2 * n)
    return rows, cols, row % 8, col % n


def cut(source, channel, place, n):
    rows, cols, down, across = place
    groups = n // 8
    lane = lax.broadcasted_iota(jnp.int32, (groups + 1, 8, n), 2)
    line = lax.broadcasted_iota(jnp.int32, (groups, 8, n), 1)
    wide = source[channel, rows, cols]
    turn = (n - across) % n
    first = pltpu.roll(wide[:, :n].reshape(groups + 1, 8, n), turn, 2)
    second = pltpu.roll(wide[:, n:].reshape(groups + 1, 8, n), turn, 2)
    tall = pltpu.roll(jnp.where(lane < n - across, first, second), (8 - down) % 8, 1)
    return jnp.where(line < 8 - down, tall[:groups], tall[1:]).reshape(n, n)


def deposit(target, channel, place, value):
    rows, cols, down, across = place
    n = value.shape[0]
    groups = n // 8
    lane = lax.broadcasted_iota(jnp.int32, (groups + 1, 8, n), 2)
    line = lax.broadcasted_iota(jnp.int32, (groups + 1, 8, n), 1)
    turned = pltpu.roll(value.reshape(groups, 8, n), down, 1)
    blank = jnp.zeros((1, 8, n), F32)
    tall = jnp.where(line >= down, jnp.concatenate([turned, blank], 0), jnp.concatenate([blank, turned], 0))
    tall = pltpu.roll(tall, across, 2)
    zero = jnp.zeros_like(tall)
    first = jnp.where(lane >= across, tall, zero).reshape(n + 8, n)
    second = jnp.where(lane < across, tall, zero).reshape(n + 8, n)
    target[channel, rows, cols] += jnp.concatenate([first, second], 1)


def cut_pair(source, place, n):
    return cut(source, 0, place, n), cut(source, 1, place, n)


def deposit_pair(target, place, terms):
    for channel in range(2):
        deposit(target[channel], 0, place, summed([term[channel] for term in terms]))


def keep(target, position, modes):
    for m, (re, im) in enumerate(modes):
        target[position, m, 0] = re
        target[position, m, 1] = im


def kept(source, position):
    return [(source[position, m, 0], source[position, m, 1]) for m in range(source.shape[1])]


def groups_of(count):
    return [range(k, min(k + GROUP, count)) for k in range(0, count, GROUP)]


def join(extended, tile, right, lower, corner):
    t = tile.shape[-1]
    extended[:, :t, :t] = tile[...]
    extended[:, :t, t:] = right[...]
    extended[:, t:, :t] = lower[...]
    extended[:, t:, t:] = corner[...]


def part_ways(total, own, right, lower, corner):
    t = own.shape[-1]
    for channel, plane in enumerate(total):
        own[channel] = plane[0, :t, :t]
        right[channel] = plane[0, :t, t:]
        lower[channel] = plane[0, t:, :t]
        corner[channel] = plane[0, t:, t:]


def pack_kernel(objects, tile, lower0, corner, right0, sems):
    n = corner.shape[-1]
    pieces = (
        (objects.at[:, :, pl.ds(0, n), pl.ds(0, n)], corner),
        (objects.at[0, :, pl.ds(0, n), :], lower0),
        (objects.at[0, :, :, pl.ds(0, n)], right0),
        (objects, tile),
    )
    copies = [pltpu.make_async_copy(piece, out, sems.at[i]) for i, (piece, out) in enumerate(pieces)]
    for copy in copies:
        copy.start()
    for copy in copies:
        copy.wait()


def stage_kernel(tile, lower1):
    lower1[...] = tile[1, :, : lower1.shape[-2], :]


def factor_kernel(*refs):
    tile, phase, table, out, table_out, right1 = refs[-6:]
    probes = refs[:-6]
    for m, probe in enumerate(probes):
        out[m] = probe[...]
    out[len(probes), 0] = jnp.cos(phase[...])
    out[len(probes), 1] = jnp.sin(phase[...])
    table_out[...] = table[...]
    right1[...] = tile[1, :, :, : right1.shape[-1]]


def factors_of(factors):
    pairs = [(factors[m, 0], factors[m, 1]) for m in range(factors.shape[0])]
    return pairs[:-1], pairs[-1]


def middle_kernel(offsets, objects, right, lower, corner, factors, table, middle, extended):
    n = corner.shape[-1]
    join(extended, objects.at[0], right, lower, corner.at[0])
    probes, spread = factors_of(factors)
    for group in groups_of(offsets.shape[0]):
        windows = [cut_pair(extended, place_of(offsets, k, n), n) for k in group]
        waves = [[times(p, window) for p in probes] for window in windows]
        waves = [fourier(wave, FORWARD, table) for wave in waves]
        waves = [[times(w, spread) for w in wave] for wave in waves]
        waves = [fourier(wave, INVERSE, table) for wave in waves]
        for k, wave in zip(group, waves):
            keep(middle, k, wave)


def second_kernel(
    offsets, objects, right, lower, corner, middle, measured, table,
    back, own, rim_right, rim_lower, rim_corner, extended, *total,
):
    n = corner.shape[-1]
    join(extended, objects.at[1], right, lower, corner.at[1])
    for plane in total:
        plane[...] = jnp.zeros_like(plane)
    for group in groups_of(offsets.shape[0]):
        windows = [cut_pair(extended, place_of(offsets, k, n), n) for k in group]
        waves = [kept(middle, k) for k in group]
        far = [[times(w, window) for w in wave] for wave, window in zip(waves, windows)]
        far = [fourier(wave, FORWARD, table) for wave in far]
        grads = []
        for k, wave in zip(group, far):
            resid = 4.0 * (summed([re * re + im * im for re, im in wave]) - measured[k])
            grads.append([(resid * re, resid * im) for re, im in wave])
        grads = [fourier(grad, INVERSE, table) for grad in grads]
        for k, grad, window in zip(group, grads, windows):
            keep(back, k, [times_conj(g, window) for g in grad])
        for k, grad, wave in zip(group, grads, waves):
            deposit_pair(total, place_of(offsets, k, n), [times_conj(g, w) for g, w in zip(grad, wave)])
    part_ways(total, own, rim_right, rim_lower, rim_corner)


def first_kernel(
    offsets, back, factors, table, other_right, other_corner, own, rim_right, rim_lower, rim_corner, *total
):
    n = rim_corner.shape[-1]
    probes, spread = factors_of(factors)
    for plane in total:
        plane[...] = jnp.zeros_like(plane)
    rim_right[1] = other_right[...]
    rim_corner[1] = other_corner[...]
    for group in groups_of(offsets.shape[0]):
        waves = [fourier(kept(back, k), FORWARD, table) for k in group]
        waves = [[times_conj(w, spread) for w in wave] for wave in waves]
        waves = [fourier(wave, INVERSE, table) for wave in waves]
        for k, wave in zip(group, waves):
            deposit_pair(total, place_of(offsets, k, n), [times_conj(w, p) for w, p in zip(wave, probes)])
    part_ways(total, own, rim_right.at[0], rim_lower, rim_corner.at[0])


def add_lower_kernel(own, lower, out):
    n = lower.shape[-2]
    out[:, n:] = own[:, n:]
    out[:, :n] = own[:, :n] + lower[...]


def write_kernel(own0, own1, out):
    out[0] = own0[...]
    out[1] = own1[...]


def finish_kernel(written, own0, own1, right, corner, out, left, sem):
    n = right.shape[-1]
    for s, own in enumerate((own0, own1)):
        left[s] = own[:, :, :n] + right[s]
    left[:, :, :n, :] += corner[...]
    copy = pltpu.make_async_copy(left, out.at[:, :, :, pl.ds(0, n)], sem)
    copy.start()
    copy.wait()


def cost(transforms, n):
    return pl.CostEstimate(flops=transforms * 24 * n * n * n, bytes_accessed=1 << 22, transcendentals=0)


def on_device(objects, probes, phase, offsets, measured):
    slices, _, t, _ = objects.shape
    n = probes.shape[2]
    reach = t + n
    mode_count = lax.axis_size("mode")
    starts, targets = offsets[0, 0], measured[0, 0]
    count = starts.shape[0]
    shape = lambda *dims: jax.ShapeDtypeStruct(dims, F32)
    params = pltpu.CompilerParams(vmem_limit_bytes=24 << 20)
    small = pltpu.CompilerParams(vmem_limit_bytes=8 << 20)
    rim_right, rim_lower, rim_corner = shape(slices, 2, t, n), shape(2, n, t), shape(slices, 2, n, n)

    tile, lower0, corner, right0 = pl.pallas_call(
        pack_kernel,
        out_shape=(shape(*objects.shape), rim_lower, rim_corner, shape(2, t, n)),
        in_specs=[pl.BlockSpec(memory_space=pltpu.HBM)],
        out_specs=(VMEM,) * 4,
        scratch_shapes=[pltpu.SemaphoreType.DMA((4,))],
        compiler_params=small,
    )(objects)
    lower0 = passed_along(lower0, "row", -1)
    corner = passed_across(corner, -1)
    right0 = passed_along(right0, "col", -1)
    received = []
    for by in range(1, mode_count):
        received.append(lax.ppermute(probes, "mode", [(i, (i + by) % mode_count) for i in range(mode_count)])[0])

    lower1 = pl.pallas_call(
        stage_kernel, out_shape=rim_lower, in_specs=[VMEM], out_specs=VMEM, compiler_params=small
    )(tile)
    lower1 = passed_along(lower1, "row", -1)
    table = tables(n)
    factors, table, right1 = pl.pallas_call(
        factor_kernel,
        out_shape=(
            shape(mode_count + 1, 2, n, n),
            jax.ShapeDtypeStruct(table.shape, table.dtype),
            shape(2, t, n),
        ),
        in_specs=[VMEM] * (mode_count + 3),
        out_specs=(VMEM,) * 3,
        compiler_params=small,
    )(probes[0], *received, tile, phase, table)
    right1 = passed_along(right1, "col", -1)
    waves = shape(count, mode_count, 2, n, n)
    window_area = pltpu.VMEM((2, reach, reach), F32)
    planes = [pltpu.VMEM((1, reach, reach), F32)] * 2
    middle = pl.pallas_call(
        middle_kernel,
        out_shape=waves,
        in_specs=[SMEM] + [VMEM] * 6,
        out_specs=VMEM,
        scratch_shapes=[window_area],
        compiler_params=params,
        cost_estimate=cost(12 * count * mode_count, n),
    )(starts, tile, right0, lower0, corner, factors, table)

    back, own1, grad_right1, grad_lower1, grad_corner1 = pl.pallas_call(
        second_kernel,
        out_shape=(waves, shape(2, t, t), shape(2, t, n), rim_lower, shape(2, n, n)),
        in_specs=[SMEM] + [VMEM] * 7,
        out_specs=(VMEM,) * 5,
        scratch_shapes=[window_area, *planes],
        compiler_params=params,
        cost_estimate=cost(6 * count * mode_count, n),
    )(starts, tile, right1, lower1, corner, middle, targets, table)
    grad_lower1 = passed_along(grad_lower1, "row", 1)
    own0, grad_right, grad_lower0, grad_corner = pl.pallas_call(
        first_kernel,
        out_shape=(shape(2, t, t), rim_right, rim_lower, rim_corner),
        in_specs=[SMEM] + [VMEM] * 5,
        out_specs=(VMEM,) * 4,
        scratch_shapes=planes,
        compiler_params=params,
        cost_estimate=cost(6 * count * mode_count, n),
    )(starts, back, factors, table, grad_right1, grad_corner1)
    grad_lower0 = passed_along(grad_lower0, "row", 1)
    grad_right = passed_along(grad_right, "col", 1)
    grad_corner = passed_across(grad_corner, 1)

    def with_lower(own, lower, weight):
        return pl.pallas_call(
            add_lower_kernel,
            out_shape=shape(2, t, t),
            in_specs=[VMEM] * 2,
            out_specs=VMEM,
            input_output_aliases={0: 0},
            compiler_params=small,
            cost_estimate=cost(weight, n),
        )(own, lower)

    own1 = with_lower(own1, grad_lower1, 20)
    own0 = with_lower(own0, grad_lower0, 90)
    written = pl.pallas_call(
        write_kernel,
        out_shape=shape(*objects.shape),
        in_specs=[VMEM] * 2,
        out_specs=VMEM,
        compiler_params=small,
        cost_estimate=cost(0, n),
    )(own0, own1)
    return pl.pallas_call(
        finish_kernel,
        out_shape=shape(*objects.shape),
        in_specs=[pl.BlockSpec(memory_space=pl.ANY)] + [VMEM] * 4,
        out_specs=pl.BlockSpec(memory_space=pl.ANY),
        scratch_shapes=[pltpu.VMEM((slices, 2, t, n), F32), pltpu.SemaphoreType.DMA],
        input_output_aliases={0: 0},
        compiler_params=small,
    )(written, own0, own1, grad_right, grad_corner)


def solution(mesh):
    placed = (
        P(None, None, "row", "col"),
        P("mode", None, None, None),
        P(),
        P("row", "col", None, None),
        P("row", "col", None, None, None),
    )
    return jax.shard_map(
        on_device,
        mesh=mesh,
        in_specs=placed,
        out_specs=P(None, None, "row", "col"),
        check_vma=False,
    )
```

```python
import functools
import math

import jax
import jax.numpy as jnp
import numpy as np
from jax import lax
from jax.experimental import pallas as pl
from jax.experimental.pallas import tpu as pltpu
from jax.sharding import PartitionSpec as P

F32 = jnp.float32
BF16 = jnp.bfloat16
FORWARD, INVERSE = 0, 1
GROUP = 4
VMEM = pl.BlockSpec(memory_space=pltpu.VMEM)
SMEM = pl.BlockSpec(memory_space=pltpu.SMEM)


def passed_along(value, axis, by):
    count = lax.axis_size(axis)
    pairs = [(i, i + by) for i in range(count) if 0 <= i + by < count]
    return lax.ppermute(value, axis, pairs)


def passed_across(value, by):
    rows, cols = lax.axis_size("row"), lax.axis_size("col")
    pairs = [
        (r * cols + c, (r + by) * cols + c + by)
        for r in range(rows)
        for c in range(cols)
        if 0 <= r + by < rows and 0 <= c + by < cols
    ]
    return lax.ppermute(value, ("row", "col"), pairs)


def tables(length):
    counter = np.arange(length)
    angle = (counter[:, None] * counter[None, :] % length) * (2.0 * math.pi / length)
    cos, sin = np.cos(angle) / math.sqrt(length), np.sin(angle) / math.sqrt(length)
    forward = np.block([[cos, -sin], [sin, cos]])
    kept = []
    for table in (forward, forward.T):
        high = table.astype(jnp.bfloat16)
        kept.append(np.stack([high, (table - high.astype(np.float64)).astype(jnp.bfloat16)]))
    return jnp.asarray(np.stack(kept))


def parts(value):
    high = value.astype(BF16)
    return high, (value - high.astype(F32)).astype(BF16)


def fourier(modes, way, table):
    n = modes[0][0].shape[0]
    right_high, right_low = table[way, 0], table[way, 1]
    left_high, left_low = table[1 - way, 0], table[1 - way, 1]
    high, low = parts(jnp.concatenate([jnp.concatenate(pair, 1) for pair in modes], 0))
    rows = jnp.dot(
        jnp.concatenate([high, low, high], 1),
        jnp.concatenate([right_high, right_high, right_low], 0),
        preferred_element_type=F32,
    )
    stacked = [
        jnp.concatenate([rows[i * n : (i + 1) * n, :n], rows[i * n : (i + 1) * n, n:]], 0) for i in range(len(modes))
    ]
    high, low = parts(jnp.concatenate(stacked, 1))
    both = jnp.dot(
        jnp.concatenate([left_high, left_high, left_low], 1),
        jnp.concatenate([high, low, high], 0),
        preferred_element_type=F32,
    )
    return [(both[:n, i * n : (i + 1) * n], both[n:, i * n : (i + 1) * n]) for i in range(len(modes))]


def times(a, b):
    return a[0] * b[0] - a[1] * b[1], a[0] * b[1] + a[1] * b[0]


def times_conj(a, b):
    return a[0] * b[0] + a[1] * b[1], a[1] * b[0] - a[0] * b[1]


def summed(values):
    return functools.reduce(lambda a, b: a + b, values)


def place_of(offsets, position, n):
    row, col = offsets[position, 0], offsets[position, 1]
    rows = pl.ds(pl.multiple_of(row // 8 * 8, 8), n + 8)
    cols = pl.ds(pl.multiple_of(col // n * n, n), 2 * n)
    return rows, cols, row % 8, col % n


def cut(source, channel, place, n):
    rows, cols, down, across = place
    groups = n // 8
    lane = lax.broadcasted_iota(jnp.int32, (groups + 1, 8, n), 2)
    line = lax.broadcasted_iota(jnp.int32, (groups, 8, n), 1)
    wide = source[channel, rows, cols]
    turn = (n - across) % n
    first = pltpu.roll(wide[:, :n].reshape(groups + 1, 8, n), turn, 2)
    second = pltpu.roll(wide[:, n:].reshape(groups + 1, 8, n), turn, 2)
    tall = pltpu.roll(jnp.where(lane < n - across, first, second), (8 - down) % 8, 1)
    return jnp.where(line < 8 - down, tall[:groups], tall[1:]).reshape(n, n)


def deposit(target, channel, place, value):
    rows, cols, down, across = place
    n = value.shape[0]
    groups = n // 8
    lane = lax.broadcasted_iota(jnp.int32, (groups + 1, 8, n), 2)
    line = lax.broadcasted_iota(jnp.int32, (groups + 1, 8, n), 1)
    turned = pltpu.roll(value.reshape(groups, 8, n), down, 1)
    blank = jnp.zeros((1, 8, n), F32)
    tall = jnp.where(line >= down, jnp.concatenate([turned, blank], 0), jnp.concatenate([blank, turned], 0))
    tall = pltpu.roll(tall, across, 2)
    zero = jnp.zeros_like(tall)
    first = jnp.where(lane >= across, tall, zero).reshape(n + 8, n)
    second = jnp.where(lane < across, tall, zero).reshape(n + 8, n)
    target[channel, rows, cols] += jnp.concatenate([first, second], 1)


def cut_pair(source, place, n):
    return cut(source, 0, place, n), cut(source, 1, place, n)


def deposit_pair(target, place, terms):
    for channel in range(2):
        deposit(target, channel, place, summed([term[channel] for term in terms]))


def keep(target, position, modes):
    for m, (re, im) in enumerate(modes):
        target[position, m, 0] = re
        target[position, m, 1] = im


def kept(source, position):
    return [(source[position, m, 0], source[position, m, 1]) for m in range(source.shape[1])]


def groups_of(count):
    return [range(k, min(k + GROUP, count)) for k in range(0, count, GROUP)]


def join(extended, tile, right, lower, corner):
    t = tile.shape[-1]
    extended[:, :t, :t] = tile[...]
    extended[:, :t, t:] = right[...]
    extended[:, t:, :t] = lower[...]
    extended[:, t:, t:] = corner[...]


def part_ways(total, own, right, lower, corner):
    t = own.shape[-1]
    own[...] = total[:, :t, :t]
    right[...] = total[:, :t, t:]
    lower[...] = total[:, t:, :t]
    corner[...] = total[:, t:, t:]


def pack_kernel(objects, tile, lower0, corner, right0):
    n = corner.shape[-1]
    lower0[...] = objects[0, :, :n, :]
    corner[...] = objects[:, :, :n, :n]
    right0[...] = objects[0, :, :, :n]
    tile[...] = objects[...]


def stage_kernel(tile, lower1):
    lower1[...] = tile[1, :, : lower1.shape[-2], :]


def factor_kernel(*refs):
    tile, phase, table, out, table_out, right1 = refs[-6:]
    probes = refs[:-6]
    for m, probe in enumerate(probes):
        out[m] = probe[...]
    out[len(probes), 0] = jnp.cos(phase[...])
    out[len(probes), 1] = jnp.sin(phase[...])
    table_out[...] = table[...]
    right1[...] = tile[1, :, :, : right1.shape[-1]]


def factors_of(factors):
    pairs = [(factors[m, 0], factors[m, 1]) for m in range(factors.shape[0])]
    return pairs[:-1], pairs[-1]


def middle_kernel(offsets, objects, right, lower, corner, factors, table, middle, extended):
    n = corner.shape[-1]
    join(extended, objects.at[0], right, lower, corner.at[0])
    probes, spread = factors_of(factors)
    for group in groups_of(offsets.shape[0]):
        windows = [cut_pair(extended, place_of(offsets, k, n), n) for k in group]
        waves = [[times(p, window) for p in probes] for window in windows]
        waves = [fourier(wave, FORWARD, table) for wave in waves]
        waves = [[times(w, spread) for w in wave] for wave in waves]
        waves = [fourier(wave, INVERSE, table) for wave in waves]
        for k, wave in zip(group, waves):
            keep(middle, k, wave)


def second_kernel(
    offsets, objects, right, lower, corner, middle, measured, table,
    back, own, rim_right, rim_lower, rim_corner, extended, total,
):
    n = corner.shape[-1]
    join(extended, objects.at[1], right, lower, corner.at[1])
    total[...] = jnp.zeros_like(total)
    for group in groups_of(offsets.shape[0]):
        windows = [cut_pair(extended, place_of(offsets, k, n), n) for k in group]
        waves = [kept(middle, k) for k in group]
        far = [[times(w, window) for w in wave] for wave, window in zip(waves, windows)]
        far = [fourier(wave, FORWARD, table) for wave in far]
        grads = []
        for k, wave in zip(group, far):
            resid = 4.0 * (summed([re * re + im * im for re, im in wave]) - measured[k])
            grads.append([(resid * re, resid * im) for re, im in wave])
        grads = [fourier(grad, INVERSE, table) for grad in grads]
        for k, grad, window in zip(group, grads, windows):
            keep(back, k, [times_conj(g, window) for g in grad])
        for k, grad, wave in zip(group, grads, waves):
            deposit_pair(total, place_of(offsets, k, n), [times_conj(g, w) for g, w in zip(grad, wave)])
    part_ways(total, own, rim_right, rim_lower, rim_corner)


def first_kernel(
    offsets, back, factors, table, other_right, other_corner, own, rim_right, rim_lower, rim_corner, total
):
    n = rim_corner.shape[-1]
    probes, spread = factors_of(factors)
    total[...] = jnp.zeros_like(total)
    rim_right[1] = other_right[...]
    rim_corner[1] = other_corner[...]
    for group in groups_of(offsets.shape[0]):
        waves = [fourier(kept(back, k), FORWARD, table) for k in group]
        waves = [[times_conj(w, spread) for w in wave] for wave in waves]
        waves = [fourier(wave, INVERSE, table) for wave in waves]
        for k, wave in zip(group, waves):
            deposit_pair(total, place_of(offsets, k, n), [times_conj(w, p) for w, p in zip(wave, probes)])
    part_ways(total, own, rim_right.at[0], rim_lower, rim_corner.at[0])


def add_lower_kernel(own, lower, out):
    n = lower.shape[-2]
    out[:, n:] = own[:, n:]
    out[:, :n] = own[:, :n] + lower[...]


def combine_kernel(own0, own1, right, corner, out):
    n = corner.shape[-1]
    out[0] = own0[...]
    out[1] = own1[...]
    for s in range(out.shape[0]):
        out[s, :, :, :n] += right[s]
        out[s, :, :n, :n] += corner[s]


def cost(transforms, n):
    return pl.CostEstimate(flops=transforms * 24 * n * n * n, bytes_accessed=1 << 22, transcendentals=0)


def on_device(objects, probes, phase, offsets, measured):
    slices, _, t, _ = objects.shape
    n = probes.shape[2]
    reach = t + n
    mode_count = lax.axis_size("mode")
    starts, targets = offsets[0, 0], measured[0, 0]
    count = starts.shape[0]
    shape = lambda *dims: jax.ShapeDtypeStruct(dims, F32)
    params = pltpu.CompilerParams(vmem_limit_bytes=24 << 20)
    small = pltpu.CompilerParams(vmem_limit_bytes=8 << 20)
    rim_right, rim_lower, rim_corner = shape(slices, 2, t, n), shape(2, n, t), shape(slices, 2, n, n)

    tile, lower0, corner, right0 = pl.pallas_call(
        pack_kernel,
        out_shape=(shape(*objects.shape), rim_lower, rim_corner, shape(2, t, n)),
        in_specs=[VMEM],
        out_specs=(VMEM,) * 4,
        compiler_params=small,
    )(objects)
    lower0 = passed_along(lower0, "row", -1)
    corner = passed_across(corner, -1)
    right0 = passed_along(right0, "col", -1)
    received = []
    for by in range(1, mode_count):
        received.append(lax.ppermute(probes, "mode", [(i, (i + by) % mode_count) for i in range(mode_count)])[0])

    lower1 = pl.pallas_call(
        stage_kernel, out_shape=rim_lower, in_specs=[VMEM], out_specs=VMEM, compiler_params=small
    )(tile)
    lower1 = passed_along(lower1, "row", -1)
    table = tables(n)
    factors, table, right1 = pl.pallas_call(
        factor_kernel,
        out_shape=(
            shape(mode_count + 1, 2, n, n),
            jax.ShapeDtypeStruct(table.shape, table.dtype),
            shape(2, t, n),
        ),
        in_specs=[VMEM] * (mode_count + 3),
        out_specs=(VMEM,) * 3,
        compiler_params=small,
    )(probes[0], *received, tile, phase, table)
    right1 = passed_along(right1, "col", -1)
    waves = shape(count, mode_count, 2, n, n)
    window_area = pltpu.VMEM((2, reach, reach), F32)
    middle = pl.pallas_call(
        middle_kernel,
        out_shape=waves,
        in_specs=[SMEM] + [VMEM] * 6,
        out_specs=VMEM,
        scratch_shapes=[window_area],
        compiler_params=params,
        cost_estimate=cost(12 * count * mode_count, n),
    )(starts, tile, right0, lower0, corner, factors, table)

    back, own1, grad_right1, grad_lower1, grad_corner1 = pl.pallas_call(
        second_kernel,
        out_shape=(waves, shape(2, t, t), shape(2, t, n), rim_lower, shape(2, n, n)),
        in_specs=[SMEM] + [VMEM] * 7,
        out_specs=(VMEM,) * 5,
        scratch_shapes=[window_area] * 2,
        compiler_params=params,
        cost_estimate=cost(6 * count * mode_count, n),
    )(starts, tile, right1, lower1, corner, middle, targets, table)
    grad_lower1 = passed_along(grad_lower1, "row", 1)
    own0, grad_right, grad_lower0, grad_corner = pl.pallas_call(
        first_kernel,
        out_shape=(shape(2, t, t), rim_right, rim_lower, rim_corner),
        in_specs=[SMEM] + [VMEM] * 5,
        out_specs=(VMEM,) * 4,
        scratch_shapes=[window_area],
        compiler_params=params,
        cost_estimate=cost(6 * count * mode_count, n),
    )(starts, back, factors, table, grad_right1, grad_corner1)
    grad_lower0 = passed_along(grad_lower0, "row", 1)
    grad_right = passed_along(grad_right, "col", 1)
    grad_corner = passed_across(grad_corner, 1)

    def with_lower(own, lower, weight):
        return pl.pallas_call(
            add_lower_kernel,
            out_shape=shape(2, t, t),
            in_specs=[VMEM] * 2,
            out_specs=VMEM,
            input_output_aliases={0: 0},
            compiler_params=small,
            cost_estimate=cost(weight, n),
        )(own, lower)

    own1 = with_lower(own1, grad_lower1, 64)
    own0 = with_lower(own0, grad_lower0, 0)
    return pl.pallas_call(
        combine_kernel,
        out_shape=jax.ShapeDtypeStruct(objects.shape, F32),
        in_specs=[VMEM] * 4,
        out_specs=VMEM,
        compiler_params=small,
    )(own0, own1, grad_right, grad_corner)


def solution(mesh):
    placed = (
        P(None, None, "row", "col"),
        P("mode", None, None, None),
        P(),
        P("row", "col", None, None),
        P("row", "col", None, None, None),
    )
    return jax.shard_map(
        on_device,
        mesh=mesh,
        in_specs=placed,
        out_specs=P(None, None, "row", "col"),
        check_vma=False,
    )
```

```python
import functools
import math

import jax
import jax.numpy as jnp
import numpy as np
from jax import lax
from jax.experimental import pallas as pl
from jax.experimental.pallas import tpu as pltpu
from jax.sharding import PartitionSpec as P

F32 = jnp.float32
BF16 = jnp.bfloat16
FORWARD, INVERSE = 0, 1
GROUP = 4
VMEM = pl.BlockSpec(memory_space=pltpu.VMEM)
SMEM = pl.BlockSpec(memory_space=pltpu.SMEM)


def passed_along(value, axis, by):
    count = lax.axis_size(axis)
    pairs = [(i, i + by) for i in range(count) if 0 <= i + by < count]
    return lax.ppermute(value, axis, pairs)


def passed_round(value, by):
    count = lax.axis_size("mode")
    return lax.ppermute(value, "mode", [(i, (i + by) % count) for i in range(count)])


def passed_across(value, by):
    rows, cols = lax.axis_size("row"), lax.axis_size("col")
    pairs = [
        (r * cols + c, (r + by) * cols + c + by)
        for r in range(rows)
        for c in range(cols)
        if 0 <= r + by < rows and 0 <= c + by < cols
    ]
    return lax.ppermute(value, ("row", "col"), pairs)


def tables(length):
    counter = np.arange(length)
    angle = (counter[:, None] * counter[None, :] % length) * (2.0 * math.pi / length)
    cos, sin = np.cos(angle) / math.sqrt(length), np.sin(angle) / math.sqrt(length)
    forward = np.block([[cos, -sin], [sin, cos]])
    kept = []
    for table in (forward, forward.T):
        high = table.astype(jnp.bfloat16)
        kept.append(np.stack([high, (table - high.astype(np.float64)).astype(jnp.bfloat16)]))
    return jnp.asarray(np.stack(kept))


def parts(value):
    high = value.astype(BF16)
    return high, (value - high.astype(F32)).astype(BF16)


def fourier(modes, way, table):
    n = modes[0][0].shape[0]
    right_high, right_low = table[way, 0], table[way, 1]
    left_high, left_low = table[1 - way, 0], table[1 - way, 1]
    high, low = parts(jnp.concatenate([jnp.concatenate(pair, 1) for pair in modes], 0))
    rows = jnp.dot(
        jnp.concatenate([high, low, high], 1),
        jnp.concatenate([right_high, right_high, right_low], 0),
        preferred_element_type=F32,
    )
    stacked = [
        jnp.concatenate([rows[i * n : (i + 1) * n, :n], rows[i * n : (i + 1) * n, n:]], 0) for i in range(len(modes))
    ]
    high, low = parts(jnp.concatenate(stacked, 1))
    both = jnp.dot(
        jnp.concatenate([left_high, left_high, left_low], 1),
        jnp.concatenate([high, low, high], 0),
        preferred_element_type=F32,
    )
    return [(both[:n, i * n : (i + 1) * n], both[n:, i * n : (i + 1) * n]) for i in range(len(modes))]


def times(a, b):
    return a[0] * b[0] - a[1] * b[1], a[0] * b[1] + a[1] * b[0]


def times_conj(a, b):
    return a[0] * b[0] + a[1] * b[1], a[1] * b[0] - a[0] * b[1]


def summed(values):
    return functools.reduce(lambda a, b: a + b, values)


def place_of(offsets, position, n):
    row, col = offsets[position, 0], offsets[position, 1]
    rows = pl.ds(pl.multiple_of(row // 8 * 8, 8), n + 8)
    cols = pl.ds(pl.multiple_of(col // n * n, n), 2 * n)
    return rows, cols, row % 8, col % n


def cut(source, channel, place, n):
    rows, cols, down, across = place
    groups = n // 8
    lane = lax.broadcasted_iota(jnp.int32, (groups + 1, 8, n), 2)
    line = lax.broadcasted_iota(jnp.int32, (groups, 8, n), 1)
    wide = source[channel, rows, cols]
    turn = (n - across) % n
    first = pltpu.roll(wide[:, :n].reshape(groups + 1, 8, n), turn, 2)
    second = pltpu.roll(wide[:, n:].reshape(groups + 1, 8, n), turn, 2)
    tall = pltpu.roll(jnp.where(lane < n - across, first, second), (8 - down) % 8, 1)
    return jnp.where(line < 8 - down, tall[:groups], tall[1:]).reshape(n, n)


def deposit(target, channel, place, value):
    rows, cols, down, across = place
    n = value.shape[0]
    groups = n // 8
    lane = lax.broadcasted_iota(jnp.int32, (groups + 1, 8, n), 2)
    line = lax.broadcasted_iota(jnp.int32, (groups + 1, 8, n), 1)
    turned = pltpu.roll(value.reshape(groups, 8, n), down, 1)
    blank = jnp.zeros((1, 8, n), F32)
    tall = jnp.where(line >= down, jnp.concatenate([turned, blank], 0), jnp.concatenate([blank, turned], 0))
    tall = pltpu.roll(tall, across, 2)
    zero = jnp.zeros_like(tall)
    first = jnp.where(lane >= across, tall, zero).reshape(n + 8, n)
    second = jnp.where(lane < across, tall, zero).reshape(n + 8, n)
    target[channel, rows, cols] += jnp.concatenate([first, second], 1)


def cut_pair(source, place, n):
    return cut(source, 0, place, n), cut(source, 1, place, n)


def deposit_pair(target, place, terms):
    for channel in range(2):
        deposit(target, channel, place, summed([term[channel] for term in terms]))


def keep(target, position, modes):
    for m, (re, im) in enumerate(modes):
        target[position, m, 0] = re
        target[position, m, 1] = im


def kept(source, position):
    return [(source[position, m, 0], source[position, m, 1]) for m in range(source.shape[1])]


def groups_of(count):
    return [range(k, min(k + GROUP, count)) for k in range(0, count, GROUP)]


def share_of(rows):
    return pl.ds(pl.multiple_of(lax.axis_index("mode") * rows, 8), rows)


def join(extended, s, tile, right, lower, corner):
    t = tile.shape[-1]
    extended[:, :t, :t] = tile[s]
    extended[:, :t, t:] = right[...]
    extended[:, t:, :t] = lower[...]
    me, count, rows = lax.axis_index("mode"), len(corner), corner[0].shape[-2]
    for slot in range(count):
        steps = lax.rem(me - slot + count, count)
        value = corner[0][s]
        for by in range(1, count):
            value = jnp.where(steps == by, corner[by][s], value)
        extended[:, t + slot * rows : t + (slot + 1) * rows, t:] = value


def part_ways(total, own, right, lower, corner):
    t = own.shape[-1]
    own[...] = total[:, :t, :t]
    right[...] = total[:, :t, t:]
    lower[...] = total[:, t:, :t]
    corner[...] = total[:, t:, t:]


def pack_kernel(objects, tile, lower0, corner, right0):
    n = right0.shape[-1]
    corner[...] = objects[:, :, share_of(corner.shape[-2]), :n]
    lower0[...] = objects[0, :, :n, :]
    right0[...] = objects[0, :, :, :n]
    tile[...] = objects[...]


def stage_kernel(tile, lower1):
    lower1[...] = tile[1, :, : lower1.shape[-2], :]


def factor_kernel(*refs):
    tile, phase, table, out, table_out, right1 = refs[-6:]
    probes = refs[:-6]
    for m, probe in enumerate(probes):
        out[m] = probe[...]
    out[len(probes), 0] = jnp.cos(phase[...])
    out[len(probes), 1] = jnp.sin(phase[...])
    table_out[...] = table[...]
    right1[...] = tile[1, :, :, : right1.shape[-1]]


def factors_of(factors):
    pairs = [(factors[m, 0], factors[m, 1]) for m in range(factors.shape[0])]
    return pairs[:-1], pairs[-1]


def middle_kernel(offsets, objects, right, lower, factors, table, *refs):
    corner, (middle, extended) = refs[:-2], refs[-2:]
    n = right.shape[-1]
    join(extended, 0, objects, right, lower, corner)
    probes, spread = factors_of(factors)
    for group in groups_of(offsets.shape[0]):
        windows = [cut_pair(extended, place_of(offsets, k, n), n) for k in group]
        waves = [[times(p, window) for p in probes] for window in windows]
        waves = [fourier(wave, FORWARD, table) for wave in waves]
        waves = [[times(w, spread) for w in wave] for wave in waves]
        waves = [fourier(wave, INVERSE, table) for wave in waves]
        for k, wave in zip(group, waves):
            keep(middle, k, wave)


def second_kernel(offsets, objects, right, lower, middle, measured, table, *refs):
    corner, (back, own, rim_right, rim_lower, rim_corner, extended, total) = refs[:-7], refs[-7:]
    n = right.shape[-1]
    join(extended, 1, objects, right, lower, corner)
    total[...] = jnp.zeros_like(total)
    for group in groups_of(offsets.shape[0]):
        windows = [cut_pair(extended, place_of(offsets, k, n), n) for k in group]
        waves = [kept(middle, k) for k in group]
        far = [[times(w, window) for w in wave] for wave, window in zip(waves, windows)]
        far = [fourier(wave, FORWARD, table) for wave in far]
        grads = []
        for k, wave in zip(group, far):
            resid = 4.0 * (summed([re * re + im * im for re, im in wave]) - measured[k])
            grads.append([(resid * re, resid * im) for re, im in wave])
        grads = [fourier(grad, INVERSE, table) for grad in grads]
        for k, grad, window in zip(group, grads, windows):
            keep(back, k, [times_conj(g, window) for g in grad])
        for k, grad, wave in zip(group, grads, waves):
            deposit_pair(total, place_of(offsets, k, n), [times_conj(g, w) for g, w in zip(grad, wave)])
    part_ways(total, own, rim_right, rim_lower, rim_corner)


def first_kernel(
    offsets, back, factors, table, other_right, other_corner, own, rim_right, rim_lower, rim_corner, total
):
    n = rim_corner.shape[-1]
    probes, spread = factors_of(factors)
    total[...] = jnp.zeros_like(total)
    rim_right[1] = other_right[...]
    rim_corner[1] = other_corner[...]
    for group in groups_of(offsets.shape[0]):
        waves = [fourier(kept(back, k), FORWARD, table) for k in group]
        waves = [[times_conj(w, spread) for w in wave] for wave in waves]
        waves = [fourier(wave, INVERSE, table) for wave in waves]
        for k, wave in zip(group, waves):
            deposit_pair(total, place_of(offsets, k, n), [times_conj(w, p) for w, p in zip(wave, probes)])
    part_ways(total, own, rim_right.at[0], rim_lower, rim_corner.at[0])


def add_lower_kernel(own, lower, out):
    n = lower.shape[-2]
    out[:, n:] = own[:, n:]
    out[:, :n] = own[:, :n] + lower[...]


def add_right_kernel(own0, own1, right, out):
    n = right.shape[-1]
    for s, own in enumerate((own0, own1)):
        out[s, :, :, n:] = own[:, :, n:]
        out[s, :, :, :n] = own[:, :, :n] + right[s]


def add_corner_kernel(own, corner, out):
    n = corner.shape[-1]
    out[...] = own[...]
    out[:, :, :n, :n] += corner[...]


def cost(transforms, n):
    return pl.CostEstimate(flops=transforms * 24 * n * n * n, bytes_accessed=1 << 22, transcendentals=0)


def on_device(objects, probes, phase, offsets, measured):
    slices, _, t, _ = objects.shape
    n = probes.shape[2]
    reach = t + n
    mode_count = lax.axis_size("mode")
    starts, targets = offsets[0, 0], measured[0, 0]
    count = starts.shape[0]
    shape = lambda *dims: jax.ShapeDtypeStruct(dims, F32)
    params = pltpu.CompilerParams(vmem_limit_bytes=24 << 20)
    small = pltpu.CompilerParams(vmem_limit_bytes=8 << 20)
    rim_right, rim_lower, rim_corner = shape(slices, 2, t, n), shape(2, n, t), shape(slices, 2, n, n)

    tile, lower0, corner, right0 = pl.pallas_call(
        pack_kernel,
        out_shape=(shape(*objects.shape), rim_lower, shape(slices, 2, n // mode_count, n), shape(2, t, n)),
        in_specs=[VMEM],
        out_specs=(VMEM,) * 4,
        compiler_params=small,
    )(objects)
    lower0 = passed_along(lower0, "row", -1)
    corner = [passed_across(corner, -1)]
    right0 = passed_along(right0, "col", -1)
    received = [passed_round(probes, by)[0] for by in range(1, mode_count)]
    corner += [passed_round(corner[0], by) for by in range(1, mode_count)]
    lower1 = pl.pallas_call(
        stage_kernel, out_shape=rim_lower, in_specs=[VMEM], out_specs=VMEM, compiler_params=small
    )(tile)
    lower1 = passed_along(lower1, "row", -1)
    table = tables(n)
    factors, table, right1 = pl.pallas_call(
        factor_kernel,
        out_shape=(
            shape(mode_count + 1, 2, n, n),
            jax.ShapeDtypeStruct(table.shape, table.dtype),
            shape(2, t, n),
        ),
        in_specs=[VMEM] * (mode_count + 3),
        out_specs=(VMEM,) * 3,
        compiler_params=small,
    )(probes[0], *received, tile, phase, table)
    right1 = passed_along(right1, "col", -1)
    waves = shape(count, mode_count, 2, n, n)
    window_area = pltpu.VMEM((2, reach, reach), F32)
    middle = pl.pallas_call(
        middle_kernel,
        out_shape=waves,
        in_specs=[SMEM] + [VMEM] * (5 + mode_count),
        out_specs=VMEM,
        scratch_shapes=[window_area],
        compiler_params=params,
        cost_estimate=cost(12 * count * mode_count, n),
    )(starts, tile, right0, lower0, factors, table, *corner)

    back, own1, grad_right1, grad_lower1, grad_corner1 = pl.pallas_call(
        second_kernel,
        out_shape=(waves, shape(2, t, t), shape(2, t, n), rim_lower, shape(2, n, n)),
        in_specs=[SMEM] + [VMEM] * (6 + mode_count),
        out_specs=(VMEM,) * 5,
        scratch_shapes=[window_area] * 2,
        compiler_params=params,
        cost_estimate=cost(6 * count * mode_count, n),
    )(starts, tile, right1, lower1, middle, targets, table, *corner)
    grad_lower1 = passed_along(grad_lower1, "row", 1)
    own0, grad_right, grad_lower0, grad_corner = pl.pallas_call(
        first_kernel,
        out_shape=(shape(2, t, t), rim_right, rim_lower, rim_corner),
        in_specs=[SMEM] + [VMEM] * 5,
        out_specs=(VMEM,) * 4,
        scratch_shapes=[window_area],
        compiler_params=params,
        cost_estimate=cost(6 * count * mode_count, n),
    )(starts, back, factors, table, grad_right1, grad_corner1)
    grad_lower0 = passed_along(grad_lower0, "row", 1)
    grad_right = passed_along(grad_right, "col", 1)
    grad_corner = passed_across(grad_corner, 1)

    def with_lower(own, lower, weight):
        return pl.pallas_call(
            add_lower_kernel,
            out_shape=shape(2, t, t),
            in_specs=[VMEM] * 2,
            out_specs=VMEM,
            input_output_aliases={0: 0},
            compiler_params=small,
            cost_estimate=cost(weight, n),
        )(own, lower)

    own1 = with_lower(own1, grad_lower1, 60)
    own0 = with_lower(own0, grad_lower0, 0)
    own = pl.pallas_call(
        add_right_kernel,
        out_shape=shape(*objects.shape),
        in_specs=[VMEM] * 3,
        out_specs=VMEM,
        compiler_params=small,
        cost_estimate=cost(0, n),
    )(own0, own1, grad_right)
    return pl.pallas_call(
        add_corner_kernel,
        out_shape=shape(*objects.shape),
        in_specs=[VMEM] * 2,
        out_specs=VMEM,
        compiler_params=small,
    )(own, grad_corner)


def solution(mesh):
    placed = (
        P(None, None, "row", "col"),
        P("mode", None, None, None),
        P(),
        P("row", "col", None, None),
        P("row", "col", None, None, None),
    )
    return jax.shard_map(
        on_device,
        mesh=mesh,
        in_specs=placed,
        out_specs=P(None, None, "row", "col"),
        check_vma=False,
    )
```
